128 devices in a mesh: latent: 16 (over x_hi, y, core), row: 4 (over z), group: 2 (over x_lo).
Axes of the slice: x: 4 (x_hi: 2, x_lo: 2; x = x_hi * 2 + x_lo), y: 4, z: 4, core: 2. Of those that a mesh axis runs over, the one named last changes fastest.
Arguments:
- attn_out: bfloat16 [512, 8192], P(None, ('latent', 'group')), may hold values from -6 to 6
- out_proj: bfloat16 [8192, 8192], P(('latent', 'group'), 'row'), may hold values from -0.0625 to 0.0625
- resid: bfloat16 [512, 8192], P(None, 'row'), may hold values from -6 to 6
- enc_weight: bfloat16 [8192, 65536], P('row', ('latent', 'group')), may hold values from -0.0625 to 0.0625
- enc_bias: float32 [65536], P(('latent', 'group')), may hold values from -1 to 0.5
- dec_bias: float32 [8192], P('row'), may hold values from -3 to 3
- moment: float32 [65536], P(('latent', 'group')), may hold values from 0.001953125 to 0.05859375
Outputs:
- update: bfloat16 [8192, 65536], P('row', ('latent', 'group'))
- new_moment: float32 [65536], P(('latent', 'group'))
The draws below stay inside these ranges and needn't reach their ends.
All inputs are finite; a program needn't handle non-finite values.
Results may differ from the reference program's by a relative error of at most 0.012.
Values may be sent and summed in bfloat16 or wider, within the bound.
No kernel may reach another device: no remote copies, remote signals or barrier semaphores. Data moves between devices by JAX's collectives and lax.ppermute only.
A program may use at most 128 MiB of HBM per device.

```python
import math
import jax
import jax.numpy as jnp
from jax import lax

D = 8192
LAT = 65536
TOKENS = 512


def level_of(key, shape, cuts, low, top_value):
    def one(position, blocks):
        heights = jax.random.uniform(jax.random.fold_in(jax.random.fold_in(key, 6), position), (blocks,), jnp.float32, low / len(cuts), top_value / len(cuts))
        return jnp.repeat(jnp.exp(heights), shape[position] // blocks).reshape((-1,) + (1,) * (len(shape) - position - 1))

    factor_of = one(*cuts[0])
    for cut in cuts[1:]:
        factor_of = factor_of * one(*cut)
    return factor_of


def gaussian(key, extent, width, bound, cuts=(), kind=jnp.bfloat16):
    result = width * jax.random.normal(key, extent, jnp.float32)
    if cuts:
        result = result * level_of(key, extent, cuts, -0.22, 0.18)
    return jnp.clip(result, -bound, bound).astype(kind)


def setup_inputs(seed: int = 0) -> dict:
    splits = jax.random.split(jax.random.key(seed), 8)
    return {
        "attn_out": gaussian(splits[0], (TOKENS, D), 1.0, 6.0, ((1, 32),)),
        "out_proj": gaussian(splits[1], (D, D), D ** -0.5, 0.0625, ((0, 32), (1, 4))),
        "resid": gaussian(splits[2], (TOKENS, D), 1.0, 6.0, ((1, 4),)),
        "enc_weight": gaussian(splits[3], (D, LAT), D ** -0.5, 0.0625, ((0, 4), (1, 32))),
        "enc_bias": jnp.clip(-1.0 + 1.5 * jax.random.uniform(splits[4], (LAT,), jnp.float32) ** level_of(splits[4], (LAT,), ((0, 32),), -0.2, 0.2), -1.0, 0.5),
        "dec_bias": gaussian(splits[5], (D,), 0.5, 3.0, ((0, 4),), jnp.float32),
        "moment": jnp.clip(jnp.exp(math.log(0.05859375) - 3.4011974 * jax.random.uniform(splits[6], (LAT,), jnp.float32) ** level_of(splits[6], (LAT,), ((0, 32),), -0.2, 0.2)), 0.001953125, 0.05859375),
    }


SHARP = 4.0
SPARSITY = 2.0
BETA = 0.9

def reference(attn_out, out_proj, resid, enc_weight, enc_bias, dec_bias, moment):
    projected = jnp.dot(attn_out, out_proj, preferred_element_type=jnp.float32)
    harvested = (resid.astype(jnp.float32) + projected).astype(jnp.bfloat16)
    preact = jnp.dot(harvested, enc_weight, preferred_element_type=jnp.float32) + enc_bias
    codes = (jax.nn.softplus(SHARP * preact) / SHARP).astype(jnp.bfloat16)
    recon = lax.dot_general(codes, enc_weight, (((1,), (1,)), ((), ())), preferred_element_type=jnp.float32) + dec_bias
    recon_grad = ((recon - harvested.astype(jnp.float32)) / TOKENS).astype(jnp.bfloat16)
    feedback = jnp.dot(recon_grad, enc_weight, preferred_element_type=jnp.float32) + SPARSITY / TOKENS
    code_grad = (feedback * jax.nn.sigmoid(SHARP * preact)).astype(jnp.bfloat16)
    blocks = 16
    column_width = LAT // blocks
    grad_blocks = code_grad.reshape(TOKENS, blocks, column_width).transpose(1, 0, 2)
    code_blocks = codes.reshape(TOKENS, blocks, column_width).transpose(1, 0, 2)
    moment_blocks = moment.reshape(blocks, column_width)

    def block_update(pieces):
        grad_piece, code_piece, moment_piece = pieces
        weight_grad = lax.dot_general(harvested, grad_piece, (((0,), (0,)), ((), ())), preferred_element_type=jnp.float32)
        weight_grad = weight_grad + lax.dot_general(recon_grad, code_piece, (((0,), (0,)), ((), ())), preferred_element_type=jnp.float32)
        energy = lax.optimization_barrier(jnp.sum(weight_grad * weight_grad, axis=0)) / D
        fresh = BETA * moment_piece + (1.0 - BETA) * energy
        return ((weight_grad / jnp.sqrt(fresh)).astype(jnp.bfloat16), fresh)
    updates, moments = lax.map(block_update, (grad_blocks, code_blocks, moment_blocks))
    update = updates.transpose(1, 0, 2).reshape(D, LAT)
    return (update, moments.reshape(LAT))
```

```python
import jax
import jax.numpy as jnp
from jax import lax
from jax.sharding import Mesh
from jax.sharding import PartitionSpec as P

D = 8192

SHARP = 4.0
SPARSITY = 2.0
BETA = 0.9

PLANE = ("xh", "y", "c", "xl")
CHIPS = ("xh", "xl", "y")
SWAP = ((0, 1), (1, 0))


def contract_rows(left, right):
    return lax.dot_general(
        left, right, (((0,), (0,)), ((), ())), preferred_element_type=jnp.float32
    )


def contract_cols(left, right):
    return lax.dot_general(
        left, right, (((1,), (1,)), ((), ())), preferred_element_type=jnp.float32
    )


def matmul(left, right):
    return jnp.dot(left, right, preferred_element_type=jnp.float32)


def bf16(a):
    return a.astype(jnp.bfloat16)


def f32(a):
    return a.astype(jnp.float32)


def shift(a, k):
    return lax.ppermute(a, "z", [(i, (i + k) % 4) for i in range(4)])


def swap(a):
    return lax.ppermute(a, "c", SWAP)


def scatter_chips(part):
    got = lax.all_to_all(part, CHIPS, 0, 0, tiled=True)
    return jnp.sum(f32(got.reshape(16, 16, -1)), axis=0)


def gather_chips(shard):
    copies = jnp.broadcast_to(shard[None], (16,) + shard.shape).reshape(256, -1)
    return lax.all_to_all(copies, CHIPS, 0, 0, tiled=True)


def scatter_rows(own, other):
    total = jnp.concatenate([f32(own[:64]), f32(other[:64])])
    for r in (2, 1, 3):
        block = slice(64 * r, 64 * r + 64)
        got = jnp.concatenate([shift(own[block], r), shift(other[block], r)])
        total = total + f32(got)
    return total


def gather_rows(shard):
    got = {r: shift(shard, -r) for r in (2, 1, 3)}
    return [shard, got[1], got[2], got[3]]


def halves(blocks):
    return jnp.concatenate([b[:64] for b in blocks] + [b[64:] for b in blocks])


def body(attn_out, out_proj, resid, enc_weight, enc_bias, dec_bias, moment):
    tokens = attn_out.shape[0]
    z = lax.axis_index("z")
    core = lax.axis_index("c")
    chip = (lax.axis_index("xh") * 2 + lax.axis_index("xl")) * 4 + lax.axis_index("y")

    def rows_of(half):
        side = jnp.where(half == 0, core, 1 - core)
        return jnp.concatenate(
            [
                lax.dynamic_slice_in_dim(attn_out, ((z + r) % 4) * 128 + side * 64, 64, 0)
                for r in range(4)
            ]
        )

    theirs = swap(bf16(matmul(rows_of(1), out_proj)))
    summed = bf16(matmul(rows_of(0), out_proj) + f32(theirs))
    first = ((z + chip // 4) % 4) * 128 + core * 64 + (chip % 4) * 16
    resid_shard = lax.dynamic_slice_in_dim(resid, first, 16, 0)
    harvested_shard = bf16(f32(resid_shard) + scatter_chips(summed))
    harvested = gather_chips(harvested_shard)
    harvested_other = swap(harvested)

    preact = (
        scatter_rows(
            bf16(matmul(harvested, enc_weight)), bf16(matmul(harvested_other, enc_weight))
        )
        + enc_bias
    )
    codes = bf16(jax.nn.softplus(SHARP * preact) / SHARP)
    slopes = jax.nn.sigmoid(SHARP * preact)
    code_blocks = gather_rows(codes)

    own_parts = []
    for block in code_blocks:
        part = contract_cols(block, enc_weight)
        own_parts.append(part[:64] + f32(swap(bf16(part[64:]))))
    recon = scatter_chips(bf16(jnp.concatenate(own_parts))) + dec_bias
    grad_shard = bf16((recon - f32(harvested_shard)) / tokens)
    recon_grad = gather_chips(grad_shard)
    recon_grad_other = swap(recon_grad)

    feedback = (
        scatter_rows(
            bf16(matmul(recon_grad, enc_weight)), bf16(matmul(recon_grad_other, enc_weight))
        )
        + SPARSITY / tokens
    )
    code_grad = halves(gather_rows(bf16(feedback * slopes)))
    weight_grad = contract_rows(
        jnp.concatenate([recon_grad, recon_grad_other]), halves(code_blocks)
    ) + contract_rows(jnp.concatenate([harvested, harvested_other]), code_grad)
    energy = jnp.sum(weight_grad * weight_grad, axis=0)
    energy = (energy + shift(energy, 2)) + (shift(energy, 1) + shift(energy, 3))
    fresh = BETA * moment + (1.0 - BETA) * (energy / D)
    update = bf16(weight_grad / jnp.sqrt(fresh))
    return (update, fresh)


def solution(mesh):
    fine = Mesh(mesh.devices.reshape(2, 4, 2, 4, 2), ("xh", "y", "c", "z", "xl"))
    placed = (
        P(None, PLANE),
        P(PLANE, "z"),
        P(None, "z"),
        P("z", PLANE),
        P(PLANE),
        P("z"),
        P(PLANE),
    )
    return jax.shard_map(
        body,
        mesh=fine,
        in_specs=placed,
        out_specs=(P("z", PLANE), P(PLANE)),
        check_vma=False,
    )
```

```python
import jax
import jax.numpy as jnp
from jax import lax
from jax.sharding import Mesh
from jax.sharding import PartitionSpec as P

D = 8192

SHARP = 4.0
SPARSITY = 2.0
BETA = 0.9

PLANE = ("xh", "y", "c", "xl")
SWAP = ((0, 1), (1, 0))


def contract_rows(left, right):
    return lax.dot_general(
        left, right, (((0,), (0,)), ((), ())), preferred_element_type=jnp.float32
    )


def contract_cols(left, right):
    return lax.dot_general(
        left, right, (((1,), (1,)), ((), ())), preferred_element_type=jnp.float32
    )


def matmul(left, right):
    return jnp.dot(left, right, preferred_element_type=jnp.float32)


def bf16(a):
    return a.astype(jnp.bfloat16)


def f32(a):
    return a.astype(jnp.float32)


def shift(a, k):
    return lax.ppermute(a, "z", [(i, (i + k) % 4) for i in range(4)])


def swap(a):
    return lax.ppermute(a, "c", SWAP)


def plane_index(x, y, c):
    return (((x // 2) * 4 + y) * 2 + c) * 2 + x % 2


def hop(a, k, first):
    pairs = []
    for x in range(4):
        for y in range(4):
            for c in range(2):
                along_x = (c == 0) == first
                to = ((x + k) % 4, y) if along_x else (x, (y + k) % 4)
                pairs.append((plane_index(x, y, c), plane_index(*to, c)))
    return lax.ppermute(a, PLANE, pairs)


def take(rows, block):
    return lax.dynamic_slice_in_dim(rows, (block % 4) * 64, 64, 0)


def plane_sum(blocks):
    total = blocks[0]
    for k in (1, 3, 2):
        total = total + f32(hop(bf16(blocks[k]), k, True))
    mine = bf16(total)
    got = {k: f32(hop(mine, k, False)) for k in (1, 3, 2)}
    return (f32(mine) + got[2]) + (got[1] + got[3])


def plane_gather(mine, place):
    got = {k: hop(mine, -k, True) for k in (1, 3, 2)}
    twice = jnp.concatenate([mine, got[1], got[2], got[3]] * 2)
    return lax.dynamic_slice_in_dim(twice, ((4 - place) % 4) * 64, 256, 0)


def scatter_rows(own, other, beside=None):
    b = lambda a, r: a[64 * r : 64 * r + 64]
    one_own, three_own = shift(b(own, 2), 1), shift(b(own, 3), -1)
    three_other, one_other = shift(b(other, 2), -1), shift(b(other, 1), 1)
    send_own = bf16(f32(b(own, 1)) + f32(one_own))
    send_other = bf16(f32(b(other, 3)) + f32(three_other))
    done = None
    if beside is not None:
        operands, call = beside
        send_own, send_other, operands = lax.optimization_barrier((send_own, send_other, operands))
        done = call(*operands)
    far_own = shift(send_own, 1)
    far_other = shift(send_other, -1)
    if beside is not None:
        far_own, far_other, done = lax.optimization_barrier((far_own, far_other, done))
    total = jnp.concatenate(
        [
            f32(b(own, 0)) + f32(three_own) + f32(far_own),
            f32(b(other, 0)) + f32(one_other) + f32(far_other),
        ]
    )
    return total, done


def gather_rows(shard):
    a, b = shard[:64], shard[64:]
    three_a, one_b = shift(a, 1), shift(b, -1)
    three_b, one_a = shift(b, 1), shift(a, -1)
    three_a, one_b = lax.optimization_barrier((three_a, one_b))
    two = [shift(three_a, 1), shift(one_b, -1)]
    return [
        shard,
        jnp.concatenate([one_a, one_b]),
        jnp.concatenate(two),
        jnp.concatenate([three_a, three_b]),
    ]


def products(own, other, weight):
    first = bf16(matmul(own, weight))
    first, other = lax.optimization_barrier((first, other))
    return first, bf16(matmul(other, weight))


def interleave(own, other):
    return jnp.concatenate([a[64 * r : 64 * r + 64] for r in range(4) for a in (own, other)])


def body(attn_out, out_proj, resid, enc_weight, enc_bias, dec_bias, moment):
    tokens = attn_out.shape[0]
    z = lax.axis_index("z")
    core = lax.axis_index("c")
    x = lax.axis_index("xh") * 2 + lax.axis_index("xl")
    place = jnp.where(core == 0, x, lax.axis_index("y"))

    def rows_of(a, turn, side):
        return lax.dynamic_slice_in_dim(a, ((z + turn) % 4) * 128 + side * 64, 64, 0)

    def project(side):
        picked = [rows_of(attn_out, place + k, side) for k in range(4)]
        return matmul(jnp.concatenate(picked), out_proj)

    other_place = jnp.where(core == 0, lax.axis_index("y"), x)
    away = matmul(
        jnp.concatenate([rows_of(attn_out, other_place + k, 1 - core) for k in range(4)]), out_proj
    )
    half = project(core) + f32(swap(bf16(away)))
    weight = enc_weight
    projected = plane_sum([half[64 * k : 64 * k + 64] for k in range(4)])
    harvested_mine = bf16(f32(rows_of(resid, place, core)) + projected)
    harvested = plane_gather(harvested_mine, place)
    harvested_other = swap(harvested)

    preact = scatter_rows(*products(harvested, harvested_other, weight))[0] + enc_bias
    codes = bf16(jax.nn.softplus(SHARP * preact) / SHARP)
    slopes = jax.nn.sigmoid(SHARP * preact)
    code_blocks = gather_rows(codes)

    halves = [None] * 4
    for r in (0, 1, 3, 2):
        part = contract_cols(code_blocks[r], weight)
        halves[r] = part[:64] + f32(swap(bf16(part[64:])))
    half = jnp.concatenate(halves)
    recon = plane_sum([take(half, place + k) for k in range(4)]) + dec_bias
    grad_mine = bf16((recon - f32(harvested_mine)) / tokens)
    recon_grad = plane_gather(grad_mine, place)
    recon_grad_other = swap(recon_grad)

    feedback, partial = scatter_rows(
        *products(recon_grad, recon_grad_other, weight),
        (
            (interleave(recon_grad, recon_grad_other), jnp.concatenate(code_blocks)),
            lambda a, b: bf16(contract_rows(a, b)),
        ),
    )
    code_grad = gather_rows(bf16((feedback + SPARSITY / tokens) * slopes))
    weight_grad = f32(partial) + contract_rows(
        interleave(harvested, harvested_other), jnp.concatenate(code_grad)
    )
    energy = jnp.sum(weight_grad * weight_grad, axis=0)
    energy = (energy + shift(energy, 2)) + (shift(energy, 1) + shift(energy, 3))
    fresh = BETA * moment + (1.0 - BETA) * (energy / D)
    update = bf16(weight_grad * (1.0 / jnp.sqrt(fresh)))
    return (update, fresh)


def solution(mesh):
    fine = Mesh(mesh.devices.reshape(2, 4, 2, 4, 2), ("xh", "y", "c", "z", "xl"))
    placed = (
        P(None, PLANE),
        P(PLANE, "z"),
        P(None, "z"),
        P("z", PLANE),
        P(PLANE),
        P("z"),
        P(PLANE),
    )
    return jax.shard_map(
        body,
        mesh=fine,
        in_specs=placed,
        out_specs=(P("z", PLANE), P(PLANE)),
        check_vma=False,
    )
```

```python
import jax
import jax.numpy as jnp
from jax import lax
from jax.sharding import Mesh
from jax.sharding import PartitionSpec as P

D = 8192

SHARP = 4.0
SPARSITY = 2.0
BETA = 0.9

PLANE = ("xh", "y", "c", "xl")
SWAP = ((0, 1), (1, 0))


def contract_rows(left, right):
    return lax.dot_general(
        left, right, (((0,), (0,)), ((), ())), preferred_element_type=jnp.float32
    )


def contract_cols(left, right):
    return lax.dot_general(
        left, right, (((1,), (1,)), ((), ())), preferred_element_type=jnp.float32
    )


def matmul(left, right):
    return jnp.dot(left, right, preferred_element_type=jnp.float32)


def bf16(a):
    return a.astype(jnp.bfloat16)


def f32(a):
    return a.astype(jnp.float32)


def shift(a, k):
    return lax.ppermute(a, "z", [(i, (i + k) % 4) for i in range(4)])


def swap(a):
    return lax.ppermute(a, "c", SWAP)


def plane_index(x, y, c):
    return (((x // 2) * 4 + y) * 2 + c) * 2 + x % 2


def hop(a, k, first):
    pairs = []
    for x in range(4):
        for y in range(4):
            for c in range(2):
                along_x = (c == 0) == first
                to = ((x + k) % 4, y) if along_x else (x, (y + k) % 4)
                pairs.append((plane_index(x, y, c), plane_index(*to, c)))
    return lax.ppermute(a, PLANE, pairs)


def take(rows, block):
    return lax.dynamic_slice_in_dim(rows, (block % 4) * 64, 64, 0)


def plane_sum(blocks):
    total = blocks[0]
    for k in (1, 3, 2):
        total = total + f32(hop(bf16(blocks[k]), k, True))
    mine = bf16(total)
    got = {k: f32(hop(mine, k, False)) for k in (1, 3, 2)}
    return (f32(mine) + got[2]) + (got[1] + got[3])


def plane_gather(mine):
    got = {k: hop(mine, -k, True) for k in (1, 3, 2)}
    return jnp.concatenate([mine, got[1], got[2], got[3]])


def scatter_rows(own, other, beside=None):
    b = lambda a, r: a[r]
    one_own, three_own = shift(b(own, 2), 1), shift(b(own, 3), -1)
    three_other, one_other = shift(b(other, 2), -1), shift(b(other, 1), 1)
    send_own = bf16(f32(b(own, 1)) + f32(one_own))
    send_other = bf16(f32(b(other, 3)) + f32(three_other))
    done = None
    if beside is not None:
        operands, call = beside
        send_own, send_other, operands = lax.optimization_barrier((send_own, send_other, operands))
        done = call(*operands)
    far_own = shift(send_own, 1)
    far_other = shift(send_other, -1)
    if beside is not None:
        far_own, far_other, done = lax.optimization_barrier((far_own, far_other, done))
    total = jnp.concatenate(
        [
            f32(b(own, 0)) + f32(three_own) + f32(far_own),
            f32(b(other, 0)) + f32(one_other) + f32(far_other),
        ]
    )
    return total, done


def gather_rows(shard, operands, call):
    a, b = shard[:64], shard[64:]
    three_a, one_b = shift(a, 1), shift(b, -1)
    shard, operands = lax.optimization_barrier((shard, operands))
    done = call(shard, *operands)
    a, b, done = lax.optimization_barrier((a, b, done))
    three_b, one_a = shift(b, 1), shift(a, -1)
    three_a, one_b = lax.optimization_barrier((three_a, one_b))
    two = [shift(three_a, 1), shift(one_b, -1)]
    blocks = [
        shard,
        jnp.concatenate([one_a, one_b]),
        jnp.concatenate(two),
        jnp.concatenate([three_a, three_b]),
    ]
    return blocks, done


def by_turn(rows, place):
    return [take(rows, r - place + 4) for r in range(4)]


def products(own, other, weight, place, other_place):
    first = bf16(matmul(own, weight))
    first, other = lax.optimization_barrier((first, other))
    return by_turn(first, place), by_turn(bf16(matmul(other, weight)), other_place)


def interleave(own, other, place, other_place):
    pairs = zip(by_turn(own, place), by_turn(other, other_place))
    return jnp.concatenate([a for pair in pairs for a in pair])


def body(attn_out, out_proj, resid, enc_weight, enc_bias, dec_bias, moment):
    tokens = attn_out.shape[0]
    z = lax.axis_index("z")
    core = lax.axis_index("c")
    x = lax.axis_index("xh") * 2 + lax.axis_index("xl")
    place = jnp.where(core == 0, x, lax.axis_index("y"))

    def rows_of(a, turn, side):
        return lax.dynamic_slice_in_dim(a, ((z + turn) % 4) * 128 + side * 64, 64, 0)

    def project(side):
        picked = [rows_of(attn_out, place + k, side) for k in range(4)]
        return matmul(jnp.concatenate(picked), out_proj)

    other_place = jnp.where(core == 0, lax.axis_index("y"), x)
    away = matmul(
        jnp.concatenate([rows_of(attn_out, other_place + k, 1 - core) for k in range(4)]), out_proj
    )
    half = project(core) + f32(swap(bf16(away)))
    weight = enc_weight
    projected = plane_sum([half[64 * k : 64 * k + 64] for k in range(4)])
    harvested_mine = bf16(f32(rows_of(resid, place, core)) + projected)
    harvested = plane_gather(harvested_mine)
    harvested_other = swap(harvested)

    preact = scatter_rows(*products(harvested, harvested_other, weight, place, other_place))[0] + enc_bias
    codes = bf16(jax.nn.softplus(SHARP * preact) / SHARP)
    code_blocks, slopes = gather_rows(
        codes, (preact,), lambda shard, preact: jax.nn.sigmoid(SHARP * preact)
    )

    halves = [None] * 4
    for r in (0, 1, 3, 2):
        part = contract_cols(code_blocks[r], weight)
        halves[r] = part[:64] + f32(swap(bf16(part[64:])))
    half = jnp.concatenate(halves)
    recon = plane_sum([take(half, place + k) for k in range(4)]) + dec_bias
    grad_mine = bf16((recon - f32(harvested_mine)) / tokens)
    recon_grad = plane_gather(grad_mine)
    recon_grad_other = swap(recon_grad)

    feedback, partial = scatter_rows(
        *products(recon_grad, recon_grad_other, weight, place, other_place),
        (
            (interleave(recon_grad, recon_grad_other, place, other_place), jnp.concatenate(code_blocks)),
            lambda a, b: bf16(contract_rows(a, b)),
        ),
    )
    code_grad, _ = gather_rows(
        bf16((feedback + SPARSITY / tokens) * slopes), (), lambda shard: ()
    )
    weight_grad = f32(partial) + contract_rows(
        interleave(harvested, harvested_other, place, other_place), jnp.concatenate(code_grad))
    energy = jnp.sum(weight_grad * weight_grad, axis=0)
    weight_grad, energy = lax.optimization_barrier((weight_grad, energy))
    energy = (energy + shift(energy, 2)) + (shift(energy, 1) + shift(energy, 3))
    fresh = BETA * moment + (1.0 - BETA) * (energy / D)
    update = bf16(weight_grad * (1.0 / jnp.sqrt(fresh)))
    return (update, fresh)


def solution(mesh):
    fine = Mesh(mesh.devices.reshape(2, 4, 2, 4, 2), ("xh", "y", "c", "z", "xl"))
    placed = (
        P(None, PLANE),
        P(PLANE, "z"),
        P(None, "z"),
        P("z", PLANE),
        P(PLANE),
        P("z"),
        P(PLANE),
    )
    return jax.shard_map(
        body,
        mesh=fine,
        in_specs=placed,
        out_specs=(P("z", PLANE), P(PLANE)),
        check_vma=False,
    )
```

```python
import jax
import jax.numpy as jnp
from jax import lax
from jax.sharding import Mesh
from jax.sharding import PartitionSpec as P

D = 8192

SHARP = 4.0
SPARSITY = 2.0
BETA = 0.9

PLANE = ("xh", "y", "c", "xl")
SWAP = ((0, 1), (1, 0))


def contract_rows(left, right):
    return lax.dot_general(
        left, right, (((0,), (0,)), ((), ())), preferred_element_type=jnp.float32
    )


def contract_cols(left, right):
    return lax.dot_general(
        left, right, (((1,), (1,)), ((), ())), preferred_element_type=jnp.float32
    )


def matmul(left, right):
    return jnp.dot(left, right, preferred_element_type=jnp.float32)


def bf16(a):
    return a.astype(jnp.bfloat16)


def f32(a):
    return a.astype(jnp.float32)


def shift(a, k):
    return lax.ppermute(a, "z", [(i, (i + k) % 4) for i in range(4)])


def swap(a):
    return lax.ppermute(a, "c", SWAP)


def plane_index(x, y, c):
    return (((x // 2) * 4 + y) * 2 + c) * 2 + x % 2


def hop(a, k, first):
    pairs = []
    for x in range(4):
        for y in range(4):
            for c in range(2):
                along_x = (c == 0) == first
                to = ((x + k) % 4, y) if along_x else (x, (y + k) % 4)
                pairs.append((plane_index(x, y, c), plane_index(*to, c)))
    return lax.ppermute(a, PLANE, pairs)


def take(rows, block):
    return lax.dynamic_slice_in_dim(rows, (block % 4) * 64, 64, 0)


def plane_sum(blocks):
    total = blocks[0]
    for k in (1, 3, 2):
        total = total + f32(hop(bf16(blocks[k]), k, True))
    mine = bf16(total)
    got = {k: f32(hop(mine, k, False)) for k in (1, 3, 2)}
    return (f32(mine) + got[2]) + (got[1] + got[3])


def plane_gather(mine):
    got = {k: hop(mine, -k, True) for k in (1, 3, 2)}
    return jnp.concatenate([mine, got[1], got[2], got[3]])


def scatter_rows(own, other, beside=None):
    b = lambda a, r: a[r]
    one_own, three_own = shift(b(own, 2), 1), shift(b(own, 3), -1)
    three_other, one_other = shift(b(other, 2), -1), shift(b(other, 1), 1)
    send_own = bf16(f32(b(own, 1)) + f32(one_own))
    send_other = bf16(f32(b(other, 3)) + f32(three_other))
    done = None
    if beside is not None:
        operands, call = beside
        send_own, send_other, operands = lax.optimization_barrier((send_own, send_other, operands))
        done = call(*operands)
    far_own = shift(send_own, 1)
    far_other = shift(send_other, -1)
    if beside is not None:
        far_own, far_other, done = lax.optimization_barrier((far_own, far_other, done))
    total = jnp.concatenate(
        [
            f32(b(own, 0)) + f32(three_own) + f32(far_own),
            f32(b(other, 0)) + f32(one_other) + f32(far_other),
        ]
    )
    return total, done


def gather_rows(shard, operands, call):
    a, b = shard[:64], shard[64:]
    three_a, one_b = shift(a, 1), shift(b, -1)
    shard, operands = lax.optimization_barrier((shard, operands))
    done = call(shard, *operands)
    a, b, done = lax.optimization_barrier((a, b, done))
    three_b, one_a = shift(b, 1), shift(a, -1)
    three_a, one_b = lax.optimization_barrier((three_a, one_b))
    two = [shift(three_a, 1), shift(one_b, -1)]
    blocks = [
        shard,
        jnp.concatenate([one_a, one_b]),
        jnp.concatenate(two),
        jnp.concatenate([three_a, three_b]),
    ]
    return blocks, done


def by_turn(rows, place):
    return [take(rows, r - place + 4) for r in range(4)]


def products(own, other, weight, place, other_place, early=None):
    if early is None:
        first = bf16(matmul(own, weight))
    else:
        first = jnp.concatenate([early, bf16(matmul(own[64:], weight))])
    first, other = lax.optimization_barrier((first, other))
    return by_turn(first, place), by_turn(bf16(matmul(other, weight)), other_place)


def interleave(own, other, place, other_place):
    pairs = zip(by_turn(own, place), by_turn(other, other_place))
    return jnp.concatenate([a for pair in pairs for a in pair])


def body(attn_out, out_proj, resid, enc_weight, enc_bias, dec_bias, moment):
    tokens = attn_out.shape[0]
    z = lax.axis_index("z")
    core = lax.axis_index("c")
    x = lax.axis_index("xh") * 2 + lax.axis_index("xl")
    place = jnp.where(core == 0, x, lax.axis_index("y"))

    def rows_of(a, turn, side):
        return lax.dynamic_slice_in_dim(a, ((z + turn) % 4) * 128 + side * 64, 64, 0)

    def project(side):
        picked = [rows_of(attn_out, place + k, side) for k in range(4)]
        return matmul(jnp.concatenate(picked), out_proj)

    other_place = jnp.where(core == 0, lax.axis_index("y"), x)
    away = matmul(
        jnp.concatenate([rows_of(attn_out, other_place + k, 1 - core) for k in range(4)]), out_proj
    )
    half = project(core) + f32(swap(bf16(away)))
    weight = enc_weight
    projected = plane_sum([half[64 * k : 64 * k + 64] for k in range(4)])
    harvested_mine = bf16(f32(rows_of(resid, place, core)) + projected)
    early = bf16(matmul(harvested_mine, weight))
    harvested = plane_gather(harvested_mine)
    harvested_other = swap(harvested)

    preact = scatter_rows(*products(harvested, harvested_other, weight, place, other_place, early))[0] + enc_bias
    codes = bf16(jax.nn.softplus(SHARP * preact) / SHARP)
    code_blocks, slopes = gather_rows(
        codes, (preact,), lambda shard, preact: jax.nn.sigmoid(SHARP * preact)
    )

    halves = [None] * 4
    for r in (0, 1, 3, 2):
        part = contract_cols(code_blocks[r], weight)
        halves[r] = part[:64] + f32(swap(bf16(part[64:])))
    half = jnp.concatenate(halves)
    recon = plane_sum([take(half, place + k) for k in range(4)]) + dec_bias
    grad_mine = bf16((recon - f32(harvested_mine)) / tokens)
    recon_grad = plane_gather(grad_mine)
    recon_grad_other = swap(recon_grad)

    feedback, partial = scatter_rows(
        *products(recon_grad, recon_grad_other, weight, place, other_place),
        (
            (interleave(recon_grad, recon_grad_other, place, other_place), jnp.concatenate(code_blocks)),
            lambda a, b: bf16(contract_rows(a, b)),
        ),
    )
    code_grad, _ = gather_rows(
        bf16((feedback + SPARSITY / tokens) * slopes), (), lambda shard: ()
    )
    weight_grad = f32(partial) + contract_rows(
        interleave(harvested, harvested_other, place, other_place), jnp.concatenate(code_grad))
    energy = jnp.sum(weight_grad * weight_grad, axis=0)
    weight_grad, energy = lax.optimization_barrier((weight_grad, energy))
    energy = (energy + shift(energy, 2)) + (shift(energy, 1) + shift(energy, 3))
    fresh = BETA * moment + (1.0 - BETA) * (energy / D)
    update = bf16(weight_grad * (1.0 / jnp.sqrt(fresh)))
    return (update, fresh)


def solution(mesh):
    fine = Mesh(mesh.devices.reshape(2, 4, 2, 4, 2), ("xh", "y", "c", "z", "xl"))
    placed = (
        P(None, PLANE),
        P(PLANE, "z"),
        P(None, "z"),
        P("z", PLANE),
        P(PLANE),
        P("z"),
        P(PLANE),
    )
    return jax.shard_map(
        body,
        mesh=fine,
        in_specs=placed,
        out_specs=(P("z", PLANE), P(PLANE)),
        check_vma=False,
    )
```

```python
import jax
import jax.numpy as jnp
from jax import lax
from jax.sharding import Mesh
from jax.sharding import PartitionSpec as P

D = 8192

SHARP = 4.0
SPARSITY = 2.0
BETA = 0.9

PLANE = ("xh", "y", "c", "xl")
SWAP = ((0, 1), (1, 0))


def contract_rows(left, right):
    return lax.dot_general(
        left, right, (((0,), (0,)), ((), ())), preferred_element_type=jnp.float32
    )


def contract_cols(left, right):
    return lax.dot_general(
        left, right, (((1,), (1,)), ((), ())), preferred_element_type=jnp.float32
    )


def matmul(left, right):
    return jnp.dot(left, right, preferred_element_type=jnp.float32)


def bf16(a):
    return a.astype(jnp.bfloat16)


def f32(a):
    return a.astype(jnp.float32)


def shift(a, k):
    return lax.ppermute(a, "z", [(i, (i + k) % 4) for i in range(4)])


def swap(a):
    return lax.ppermute(a, "c", SWAP)


def plane_index(x, y, c):
    return (((x // 2) * 4 + y) * 2 + c) * 2 + x % 2


def hop(a, k, first):
    pairs = []
    for x in range(4):
        for y in range(4):
            for c in range(2):
                along_x = (c == 0) == first
                to = ((x + k) % 4, y) if along_x else (x, (y + k) % 4)
                pairs.append((plane_index(x, y, c), plane_index(*to, c)))
    return lax.ppermute(a, PLANE, pairs)


def take(rows, block):
    return lax.dynamic_slice_in_dim(rows, (block % 4) * 64, 64, 0)


def plane_sum(blocks):
    total = blocks[0]
    for k in (1, 3, 2):
        total = total + f32(hop(bf16(blocks[k]), k, True))
    mine = bf16(total)
    got = {k: f32(hop(mine, k, False)) for k in (1, 3, 2)}
    return (f32(mine) + got[2]) + (got[1] + got[3])


def plane_gather(mine):
    got = {k: hop(mine, -k, True) for k in (1, 3, 2)}
    return jnp.concatenate([mine, got[1], got[2], got[3]])


def scatter_rows(own, other, beside=None):
    b = lambda a, r: a[r]
    one_own, three_own = shift(b(own, 2), 1), shift(b(own, 3), -1)
    three_other, one_other = shift(b(other, 2), -1), shift(b(other, 1), 1)
    send_own = bf16(f32(b(own, 1)) + f32(one_own))
    send_other = bf16(f32(b(other, 3)) + f32(three_other))
    done = None
    if beside is not None:
        operands, call = beside
        send_own, send_other, operands = lax.optimization_barrier((send_own, send_other, operands))
        done = call(*operands)
    far_own = shift(send_own, 1)
    far_other = shift(send_other, -1)
    if beside is not None:
        far_own, far_other, done = lax.optimization_barrier((far_own, far_other, done))
    total = jnp.concatenate(
        [
            f32(b(own, 0)) + f32(three_own) + f32(far_own),
            f32(b(other, 0)) + f32(one_other) + f32(far_other),
        ]
    )
    return total, done


def gather_rows(shard, operands, call):
    a, b = shard[:64], shard[64:]
    three_a, one_b = shift(a, 1), shift(b, -1)
    shard, operands = lax.optimization_barrier((shard, operands))
    done = call(shard, *operands)
    a, b, done = lax.optimization_barrier((a, b, done))
    three_b, one_a = shift(b, 1), shift(a, -1)
    three_a, one_b = lax.optimization_barrier((three_a, one_b))
    two = [shift(three_a, 1), shift(one_b, -1)]
    blocks = [
        shard,
        jnp.concatenate([one_a, one_b]),
        jnp.concatenate(two),
        jnp.concatenate([three_a, three_b]),
    ]
    return blocks, done


def by_turn(rows, place):
    return [take(rows, r - place + 4) for r in range(4)]


def products(own, other, weight, place, other_place, early=None):
    if early is None:
        first = bf16(matmul(own, weight))
    else:
        first = jnp.concatenate([early, bf16(matmul(own[64:], weight))])
    first, other = lax.optimization_barrier((first, other))
    return by_turn(first, place), by_turn(bf16(matmul(other, weight)), other_place)


def interleave(own, other, place, other_place):
    pairs = zip(by_turn(own, place), by_turn(other, other_place))
    return jnp.concatenate([a for pair in pairs for a in pair])


def body(attn_out, out_proj, resid, enc_weight, enc_bias, dec_bias, moment):
    tokens = attn_out.shape[0]
    z = lax.axis_index("z")
    core = lax.axis_index("c")
    x = lax.axis_index("xh") * 2 + lax.axis_index("xl")
    place = jnp.where(core == 0, x, lax.axis_index("y"))

    def rows_of(a, turn, side):
        return lax.dynamic_slice_in_dim(a, ((z + turn) % 4) * 128 + side * 64, 64, 0)

    def project(side):
        picked = [rows_of(attn_out, place + k, side) for k in range(4)]
        return matmul(jnp.concatenate(picked), out_proj)

    other_place = jnp.where(core == 0, lax.axis_index("y"), x)
    away = matmul(
        jnp.concatenate([rows_of(attn_out, other_place + k, 1 - core) for k in range(4)]), out_proj
    )
    half = project(core) + f32(swap(bf16(away)))
    weight = enc_weight
    projected = plane_sum([half[64 * k : 64 * k + 64] for k in range(4)])
    harvested_mine = bf16(f32(rows_of(resid, place, core)) + projected)
    early = bf16(matmul(harvested_mine, weight))
    harvested = plane_gather(harvested_mine)
    harvested_other = swap(harvested)

    preact = scatter_rows(*products(harvested, harvested_other, weight, place, other_place, early))[0] + enc_bias
    codes = bf16(jax.nn.softplus(SHARP * preact) / SHARP)
    code_blocks, slopes = gather_rows(
        codes, (preact,), lambda shard, preact: jax.nn.sigmoid(SHARP * preact)
    )

    halves = [None] * 4
    for r in (0, 1, 3, 2):
        part = contract_cols(code_blocks[r], weight)
        halves[r] = part[:64] + f32(swap(bf16(part[64:])))
    half = jnp.concatenate(halves)
    recon = plane_sum([take(half, place + k) for k in range(4)]) + dec_bias
    grad_mine = bf16((recon - f32(harvested_mine)) / tokens)
    early_grad = bf16(matmul(grad_mine, weight))
    recon_grad = plane_gather(grad_mine)
    recon_grad_other = swap(recon_grad)

    feedback, partial = scatter_rows(
        *products(recon_grad, recon_grad_other, weight, place, other_place, early_grad),
        (
            (interleave(recon_grad, recon_grad_other, place, other_place), jnp.concatenate(code_blocks)),
            lambda a, b: bf16(contract_rows(a, b)),
        ),
    )
    code_grad, _ = gather_rows(
        bf16((feedback + SPARSITY / tokens) * slopes), (), lambda shard: ()
    )
    weight_grad = f32(partial) + contract_rows(
        interleave(harvested, harvested_other, place, other_place), jnp.concatenate(code_grad))
    energy = jnp.sum(weight_grad * weight_grad, axis=0)
    weight_grad, energy = lax.optimization_barrier((weight_grad, energy))
    energy = (energy + shift(energy, 2)) + (shift(energy, 1) + shift(energy, 3))
    fresh = BETA * moment + (1.0 - BETA) * (energy / D)
    update = bf16(weight_grad * (1.0 / jnp.sqrt(fresh)))
    return (update, fresh)


def solution(mesh):
    fine = Mesh(mesh.devices.reshape(2, 4, 2, 4, 2), ("xh", "y", "c", "z", "xl"))
    placed = (
        P(None, PLANE),
        P(PLANE, "z"),
        P(None, "z"),
        P("z", PLANE),
        P(PLANE),
        P("z"),
        P(PLANE),
    )
    return jax.shard_map(
        body,
        mesh=fine,
        in_specs=placed,
        out_specs=(P("z", PLANE), P(PLANE)),
        check_vma=False,
    )
```
